32 devices in a mesh: lines: 2 (over y), freq: 8 (over z, x), rows: 2 (over core).
Axes of the slice: x: 2, y: 2, z: 4, core: 2. Of those that a mesh axis runs over, the one named last changes fastest.
Arguments:
- traces: float32 [1024, 512, 1024], P(('lines', 'freq'), 'rows'), parts along dimension 0, may hold values from -6 to 6
- win_start: int32 [1024], P(('lines', 'freq')), parts along dimension 0, may hold values from 0 to 255
- win_stop: int32 [1024], P(('lines', 'freq')), parts along dimension 0, may hold values from 768 to 1024
- shot_live: int32 [1024], P(('lines', 'freq')), parts along dimension 0, may hold values 0 or 1
- recv_live: int32 [1024], P(('lines', 'rows')), parts along dimension 0, may hold values 0 or 1
- band_start: int32 [2], P('lines'), parts along dimension 0, may hold values from 1 to 511
Outputs:
- multiples: bfloat16 [2, 16, 512, 512], P(None, ('lines', 'freq'), None, 'rows'), parts along dimension 1
The draws below stay inside these ranges and needn't reach their ends.
There are 2 independent parts, one for each index of `lines`. The reference program is written for one: setup_inputs(seed, part) draws one part's arguments, and reference() takes and returns one part's arrays. A program takes and returns all parts, laid end to end along the dimension named above; each array names one. Nothing has to cross between parts.
All inputs are finite; a program needn't handle non-finite values. No bound on the sum of `shot_live` or of `recv_live` on one device may be relied on, other than what follows from the above.
Results may differ from the reference program's by a relative error of at most 0.001.
Values sent between devices are 32-bit elements; how exact they have to be, the bound alone decides.
A program may use at most 192 MiB of HBM per device.

```python
import math
import jax
import jax.numpy as jnp
from jax import lax

NS = 512
NR = 512
NT = 1024
RAMP = 32
NF = 8


def plant(drawn, stream_key, low, top_value):
    dims = drawn.shape
    index_at = [jax.random.randint(jax.random.fold_in(stream_key, axis), (), 0, dims[axis]) for axis in range(len(dims))]
    drawn = drawn.at[tuple(index_at)].set(low)
    longest = dims.index(max(dims))
    index_at[longest] = (index_at[longest] + 1) % dims[longest]
    return drawn.at[tuple(index_at)].set(top_value)


def level_of(own_key, extent, shards, least, high):
    def one(dim, blocks):
        heights = jax.random.uniform(jax.random.fold_in(jax.random.fold_in(own_key, 6), dim), (blocks,), jnp.float32, least / len(shards), high / len(shards))
        return jnp.repeat(jnp.exp(heights), extent[dim] // blocks).reshape((-1,) + (1,) * (len(extent) - dim - 1))

    loudness = one(*shards[0])
    for cut in shards[1:]:
        loudness = loudness * one(*cut)
    return loudness


def scatter_about(key, extent, spread, bound, pieces=(), held_as=jnp.bfloat16):
    array = spread * jax.random.normal(key, extent, jnp.float32)
    if pieces:
        array = array * level_of(key, extent, pieces, -0.22, 0.18)
    return jnp.clip(array, -bound, bound).astype(held_as)


def setup_inputs(seed: int = 0, part: int = 0) -> dict:
    keys = jax.random.split(jax.random.key(seed), 7)
    own_keys = jax.random.split(jax.random.fold_in(keys[6], part), 7)
    traces = scatter_about(own_keys[0], (NS, NR, NT), 1.0, 6.0, ((0, 8), (1, 2)), jnp.float32)
    win_start = plant(jax.random.randint(own_keys[1], (NS,), 0, NT // 4), jax.random.fold_in(own_keys[1], 1), 0, (NT // 4) - 1).astype(jnp.int32)
    win_stop = plant(jax.random.randint(own_keys[2], (NS,), 3 * NT // 4, NT + 1), jax.random.fold_in(own_keys[2], 1), 3 * NT // 4, NT).astype(jnp.int32)
    shot_live = plant((jax.random.randint(own_keys[3], (NS,), 0, 8) < 7).astype(jnp.int32), jax.random.fold_in(own_keys[3], 1), 0, 1)
    recv_live = plant((jax.random.randint(own_keys[4], (NR,), 0, 8) < 7).astype(jnp.int32), jax.random.fold_in(own_keys[4], 1), 0, 1)
    band_start = jax.random.randint(own_keys[5], (1,), 1, NT // 2).astype(jnp.int32)
    return dict(traces=traces, win_start=win_start, win_stop=win_stop, shot_live=shot_live, recv_live=recv_live, band_start=band_start)


def reference(traces, win_start, win_stop, shot_live, recv_live, band_start):
    times = jnp.arange(NT, dtype=jnp.float32)[None, :]
    start = win_start.astype(jnp.float32)[:, None]
    stop = win_stop.astype(jnp.float32)[:, None]
    weight = jnp.clip((times - start) / RAMP, 0.0, 1.0) * jnp.clip((stop - times) / RAMP, 0.0, 1.0)
    live = shot_live.astype(jnp.float32)[:, None] * recv_live.astype(jnp.float32)[None, :]
    blocks = 16
    shot_block = NS // blocks
    tr_blocks = traces.reshape(blocks, shot_block, NR, NT)
    we_blocks = weight.reshape(blocks, shot_block, NT)
    li_blocks = live.reshape(blocks, shot_block, NR)
    scale = 1.0 / math.sqrt(NT)
    picks = ((band_start[0] + jnp.arange(NF, dtype=jnp.int32)) % NT).astype(jnp.int32)

    def transform(items):
        block, wblock, lblock = items
        tapered = block * wblock[:, None, :] * lblock[:, :, None]
        spec = jnp.fft.fft(tapered, axis=2)
        band = jnp.take(spec, picks, axis=2)
        return jnp.stack([jnp.real(band), jnp.imag(band)]).astype(jnp.float32) * scale
    spectra = lax.map(transform, (tr_blocks, we_blocks, li_blocks))
    spectra = jnp.transpose(spectra, (1, 4, 0, 2, 3)).reshape(2, NF, NS, NR)
    upper_limit = lax.Precision.HIGHEST
    output_scale_factor = 1.0 / math.sqrt(NS)

    def predict_multiples(mats):
        real_part, imag_part = mats
        multiple_real = jnp.dot(real_part, real_part, precision=upper_limit) - jnp.dot(imag_part, imag_part, precision=upper_limit)
        multiple_imaginary = jnp.dot(real_part, imag_part, precision=upper_limit) + jnp.dot(imag_part, real_part, precision=upper_limit)
        return jnp.stack([multiple_real, multiple_imaginary]) * output_scale_factor
    result = lax.map(predict_multiples, (spectra[0], spectra[1]))
    return jnp.swapaxes(result, 0, 1).astype(jnp.bfloat16)
```

```python
import functools
import math

import jax
import jax.numpy as jnp
from jax import lax
from jax.experimental import pallas as pl
from jax.experimental.pallas import tpu as pltpu
from jax.sharding import PartitionSpec as P

RAMP = 32
SLOTS = 8
MESH = pl.DeviceIdType.MESH


def dft_table(band_start, length, count):
    times = jnp.arange(length, dtype=jnp.int32)[None, :]
    freqs = (band_start[0] + jnp.arange(count, dtype=jnp.int32)[:, None]) % length
    phase = (freqs * times % length).astype(jnp.float32) * (2.0 * math.pi / length)
    return jnp.concatenate([jnp.cos(phase), -jnp.sin(phase)], 0) * (1.0 / math.sqrt(length))


def split(x):
    high = x.astype(jnp.bfloat16)
    return high, (x - high.astype(jnp.float32)).astype(jnp.bfloat16)


def kernel(n, chunk, traces, weight, live, waves, out, table, slots, send, held, other, own, sib,
           slot_sem, send_sem, recv_sem, keep_sem, pass_sem, take_sem):
    me = lax.axis_index("freq")
    core = lax.axis_index("rows")
    shots, cols, length = traces.shape
    parts = shots // chunk

    def fetch(s):
        slot = lax.rem(s, SLOTS)
        return pltpu.make_async_copy(traces.at[s], slots.at[slot], slot_sem.at[slot])

    def remote(c, p):
        to = lax.rem(me + p, n)
        rows = pl.ds(c * chunk, chunk)
        return pltpu.make_async_remote_copy(
            send.at[:, to, rows, :], held.at[:, me, rows, :],
            send_sem.at[c, p - 1], recv_sem.at[c, p - 1],
            device_id={"freq": to}, device_id_type=MESH)

    def arrival(c, p):
        source = lax.rem(me + n - p, n)
        rows = pl.ds(c * chunk, chunk)
        return pltpu.make_async_remote_copy(
            send.at[:, source, rows, :], held.at[:, source, rows, :],
            send_sem.at[c, p - 1], recv_sem.at[c, p - 1],
            device_id={"freq": source}, device_id_type=MESH)

    def keep(c):
        rows = pl.ds(c * chunk, chunk)
        return pltpu.make_async_copy(send.at[:, me, rows, :], held.at[:, me, rows, :], keep_sem.at[c])

    def hand(c):
        rows = pl.ds(c * chunk, chunk)
        return pltpu.make_async_remote_copy(
            held.at[:, :, rows, :], other.at[:, :, rows, :], pass_sem.at[c], take_sem.at[c],
            device_id={"rows": 1 - core}, device_id_type=MESH)

    def hand_over(c):
        def land(p, carry):
            arrival(c, p).wait_recv()
            return carry
        lax.fori_loop(1, n, land, 0)
        keep(c).wait()
        hand(c).start()

    for s in range(min(SLOTS, shots)):
        fetch(s).start()

    table[:2 * n], table[2 * n:] = split(waves[...])

    barrier = pltpu.get_barrier_semaphore()

    def greet(p, carry):
        pl.semaphore_signal(barrier, inc=1, device_id={"freq": lax.rem(me + p, n)}, device_id_type=MESH)
        return carry
    lax.fori_loop(1, n, greet, 0)
    pl.semaphore_signal(barrier, inc=1, device_id={"rows": 1 - core}, device_id_type=MESH)

    def transform(s, carry):
        fetch(s).wait()
        slot = lax.rem(s, SLOTS)
        total = jnp.zeros((4 * n, cols), jnp.float32)
        step = 256
        for k in range(0, length, step):
            x = slots[slot, :, k:k + step] * weight[pl.ds(s, 1), k:k + step]
            high, low = split(x)
            part = table[:, k:k + step]
            for piece in (high, low):
                total += lax.dot_general(part, piece, (((1,), (1,)), ((), ())),
                                         preferred_element_type=jnp.float32)
        spec = (total[:2 * n] + total[2 * n:]) * live[...]
        for j in range(2 * n):
            send[j // n, j % n, pl.ds(s, 1), :] = spec[j:j + 1, :]

        @pl.when(s + SLOTS < shots)
        def _():
            fetch(s + SLOTS).start()
        return carry

    for c in range(parts):
        lax.fori_loop(c * chunk, (c + 1) * chunk, transform, 0)
        if c == 0:
            pl.semaphore_wait(barrier, n)

        def launch(p, carry):
            remote(c, p).start()
            return carry
        lax.fori_loop(1, n, launch, 0)
        keep(c).start()
        if c >= 2:
            hand_over(c - 2)
    for c in range(max(parts - 2, 0), parts):
        hand_over(c)

    def place(source_ref, target):
        for w in range(2):
            for source in range(n):
                target[w, source * shots:(source + 1) * shots, :] = source_ref[w, source]

    place(held, own)
    for c in range(parts):
        hand(c).wait_recv()
    place(other, sib)

    total_rows = n * shots
    scale = 1.0 / math.sqrt(total_rows)
    factors = []
    for half in (core, 1 - core):
        start = pl.multiple_of(half * cols, cols)
        right = jnp.concatenate([own[w, pl.ds(start, cols), :] for w in range(2)], 1)
        factors.append(split(right))
    tile = 128

    def multiply(i, carry):
        rows = pl.ds(pl.multiple_of(i * tile, tile), tile)
        sums = []
        for w in range(2):
            acc = jnp.zeros((tile, 2 * cols), jnp.float32)
            for ref, (right_high, right_low) in zip((own, sib), factors):
                high, low = split(ref[w, rows, :])
                acc += jnp.dot(high, right_high, preferred_element_type=jnp.float32)
                acc += jnp.dot(high, right_low, preferred_element_type=jnp.float32)
                acc += jnp.dot(low, right_high, preferred_element_type=jnp.float32)
            sums.append(acc)
        out[0, rows, :] = ((sums[0][:, :cols] - sums[1][:, cols:]) * scale).astype(out.dtype)
        out[1, rows, :] = ((sums[0][:, cols:] + sums[1][:, :cols]) * scale).astype(out.dtype)
        return carry
    lax.fori_loop(0, total_rows // tile, multiply, 0)

    for c in range(parts):
        def sent(p, carry):
            remote(c, p).wait_send()
            return carry
        lax.fori_loop(1, n, sent, 0)
        hand(c).wait_send()


def shards(traces, win_start, win_stop, shot_live, recv_live, band_start):
    shots, cols, length = traces.shape
    n = lax.axis_size("freq")
    times = jnp.arange(length, dtype=jnp.float32)[None, :]
    start = win_start.astype(jnp.float32)[:, None]
    stop = win_stop.astype(jnp.float32)[:, None]
    weight = jnp.clip((times - start) / RAMP, 0.0, 1.0) * jnp.clip((stop - times) / RAMP, 0.0, 1.0)
    weight = weight * shot_live.astype(jnp.float32)[:, None]
    waves = dft_table(band_start, length, n)
    chunk = min(16, shots)
    parts = shots // chunk
    block = (2, n, shots, cols)
    vmem = pl.BlockSpec(memory_space=pltpu.VMEM)
    out = pl.pallas_call(
        functools.partial(kernel, n, chunk),
        out_shape=jax.ShapeDtypeStruct((2, n * shots, cols), jnp.bfloat16),
        in_specs=[pl.BlockSpec(memory_space=pl.ANY), vmem, vmem, vmem],
        out_specs=vmem,
        scratch_shapes=[
            pltpu.VMEM((4 * n, length), jnp.bfloat16),
            pltpu.VMEM((SLOTS, cols, length), jnp.float32),
            pltpu.VMEM(block, jnp.float32),
            pltpu.VMEM(block, jnp.float32),
            pltpu.VMEM(block, jnp.float32),
            pltpu.VMEM((2, n * shots, cols), jnp.float32),
            pltpu.VMEM((2, n * shots, cols), jnp.float32),
            pltpu.SemaphoreType.DMA((SLOTS,)),
            pltpu.SemaphoreType.DMA((parts, n - 1)),
            pltpu.SemaphoreType.DMA((parts, n - 1)),
            pltpu.SemaphoreType.DMA((parts,)),
            pltpu.SemaphoreType.DMA((parts,)),
            pltpu.SemaphoreType.DMA((parts,)),
        ],
        compiler_params=pltpu.CompilerParams(
            collective_id=0, has_side_effects=True, vmem_limit_bytes=56 * 1024 * 1024),
        cost_estimate=pl.CostEstimate(flops=2 * 10**10, bytes_accessed=4 * shots * cols * length, transcendentals=0),
    )(traces, weight, recv_live.astype(jnp.float32)[None, :], waves)
    return out[:, None]


def solution(mesh):
    placed = (
        P(("lines", "freq"), "rows", None),
        P(("lines", "freq")),
        P(("lines", "freq")),
        P(("lines", "freq")),
        P(("lines", "rows")),
        P("lines"),
    )
    return jax.shard_map(
        shards,
        mesh=mesh,
        in_specs=placed,
        out_specs=P(None, ("lines", "freq"), None, "rows"),
        check_vma=False,
    )
```

```python
import functools
import math

import jax
import jax.numpy as jnp
from jax import lax
from jax.experimental import pallas as pl
from jax.experimental.pallas import tpu as pltpu
from jax.sharding import PartitionSpec as P

RAMP = 32
SLOTS = 8
MESH = pl.DeviceIdType.MESH


def split(x):
    high = x.astype(jnp.bfloat16)
    return high, (x - high.astype(jnp.float32)).astype(jnp.bfloat16)


def kernel(n, chunk, traces, win_start, win_stop, shot_live, recv_live, band_start, out, waves, slots, send, held, other, own, sib,
           slot_sem, send_sem, recv_sem, keep_sem, pass_sem, take_sem):
    me = lax.axis_index("freq")
    core = lax.axis_index("rows")
    shots, cols, length = traces.shape
    parts = shots // chunk

    def fetch(s):
        slot = lax.rem(s, SLOTS)
        return pltpu.make_async_copy(traces.at[s], slots.at[slot], slot_sem.at[slot])

    def remote(c, p):
        to = lax.rem(me + p, n)
        rows = pl.ds(c * chunk, chunk)
        return pltpu.make_async_remote_copy(
            send.at[:, to, rows, :], held.at[:, me, rows, :],
            send_sem.at[c, p - 1], recv_sem.at[c, p - 1],
            device_id={"freq": to}, device_id_type=MESH)

    def arrival(c, p):
        source = lax.rem(me + n - p, n)
        rows = pl.ds(c * chunk, chunk)
        return pltpu.make_async_remote_copy(
            send.at[:, source, rows, :], held.at[:, source, rows, :],
            send_sem.at[c, p - 1], recv_sem.at[c, p - 1],
            device_id={"freq": source}, device_id_type=MESH)

    def keep(c):
        rows = pl.ds(c * chunk, chunk)
        return pltpu.make_async_copy(send.at[:, me, rows, :], held.at[:, me, rows, :], keep_sem.at[c])

    def hand(c):
        rows = pl.ds(c * chunk, chunk)
        return pltpu.make_async_remote_copy(
            held.at[:, :, rows, :], other.at[:, :, rows, :], pass_sem.at[c], take_sem.at[c],
            device_id={"rows": 1 - core}, device_id_type=MESH)

    def hand_over(c):
        def land(p, carry):
            arrival(c, p).wait_recv()
            return carry
        lax.fori_loop(1, n, land, 0)
        keep(c).wait()
        hand(c).start()

    for s in range(min(SLOTS, shots)):
        fetch(s).start()

    row = lax.broadcasted_iota(jnp.int32, (2 * n, length), 0)
    times = lax.broadcasted_iota(jnp.int32, (2 * n, length), 1)
    sine = row >= n
    freqs = (band_start[0] + row - jnp.where(sine, n, 0)) & (length - 1)
    turns = (freqs * times + jnp.where(sine, length // 4, 0)) & (length - 1)
    waves[...] = jnp.cos(turns.astype(jnp.float32) * (2.0 * math.pi / length)) * (1.0 / math.sqrt(length))
    live = recv_live[...].astype(jnp.float32)
    clock = lax.broadcasted_iota(jnp.int32, (1, length), 1)

    barrier = pltpu.get_barrier_semaphore()

    def greet(p, carry):
        pl.semaphore_signal(barrier, inc=1, device_id={"freq": lax.rem(me + p, n)}, device_id_type=MESH)
        return carry
    lax.fori_loop(1, n, greet, 0)
    pl.semaphore_signal(barrier, inc=1, device_id={"rows": 1 - core}, device_id_type=MESH)

    def transform(s, carry):
        fetch(s).wait()
        slot = lax.rem(s, SLOTS)
        total = jnp.zeros((4 * n, cols), jnp.float32)
        rise = jnp.clip((clock - win_start[s]).astype(jnp.float32) * (1.0 / RAMP), 0.0, 1.0)
        fall = jnp.clip((win_stop[s] - clock).astype(jnp.float32) * (1.0 / RAMP), 0.0, 1.0)
        weight = rise * fall * shot_live[s].astype(jnp.float32)
        table = jnp.concatenate(split(waves[...] * weight), 0)
        step = 256
        for k in range(0, length, step):
            part = table[:, k:k + step]
            for piece in split(slots[slot, :, k:k + step]):
                total += lax.dot_general(part, piece, (((1,), (1,)), ((), ())),
                                         preferred_element_type=jnp.float32)
        spec = (total[:2 * n] + total[2 * n:]) * live
        for j in range(2 * n):
            send[j // n, j % n, pl.ds(s, 1), :] = spec[j:j + 1, :]

        @pl.when(s + SLOTS < shots)
        def _():
            fetch(s + SLOTS).start()
        return carry

    for c in range(parts):
        lax.fori_loop(c * chunk, (c + 1) * chunk, transform, 0)
        if c == 0:
            pl.semaphore_wait(barrier, n)

        def launch(p, carry):
            remote(c, p).start()
            return carry
        lax.fori_loop(1, n, launch, 0)
        keep(c).start()
        if c >= 2:
            hand_over(c - 2)
    for c in range(max(parts - 2, 0), parts):
        hand_over(c)

    def place(source_ref, target):
        for w in range(2):
            for source in range(n):
                target[w, source * shots:(source + 1) * shots, :] = source_ref[w, source]

    place(held, own)
    for c in range(parts):
        hand(c).wait_recv()
    place(other, sib)

    total_rows = n * shots
    scale = 1.0 / math.sqrt(total_rows)
    factors = []
    for half in (core, 1 - core):
        start = pl.multiple_of(half * cols, cols)
        right = jnp.concatenate([own[w, pl.ds(start, cols), :] for w in range(2)], 1)
        factors.append(split(right))
    tile = 128

    def multiply(i, carry):
        rows = pl.ds(pl.multiple_of(i * tile, tile), tile)
        sums = []
        for w in range(2):
            acc = jnp.zeros((tile, 2 * cols), jnp.float32)
            for ref, (right_high, right_low) in zip((own, sib), factors):
                high, low = split(ref[w, rows, :])
                acc += jnp.dot(high, right_high, preferred_element_type=jnp.float32)
                acc += jnp.dot(high, right_low, preferred_element_type=jnp.float32)
                acc += jnp.dot(low, right_high, preferred_element_type=jnp.float32)
            sums.append(acc)
        out[0, rows, :] = ((sums[0][:, :cols] - sums[1][:, cols:]) * scale).astype(out.dtype)
        out[1, rows, :] = ((sums[0][:, cols:] + sums[1][:, :cols]) * scale).astype(out.dtype)
        return carry
    lax.fori_loop(0, total_rows // tile, multiply, 0)

    for c in range(parts):
        def sent(p, carry):
            remote(c, p).wait_send()
            return carry
        lax.fori_loop(1, n, sent, 0)
        hand(c).wait_send()


def shards(traces, win_start, win_stop, shot_live, recv_live, band_start):
    shots, cols, length = traces.shape
    n = lax.axis_size("freq")
    chunk = min(8, shots)
    parts = shots // chunk
    block = (2, n, shots, cols)
    vmem = pl.BlockSpec(memory_space=pltpu.VMEM)
    smem = pl.BlockSpec(memory_space=pltpu.SMEM)
    out = pl.pallas_call(
        functools.partial(kernel, n, chunk),
        out_shape=jax.ShapeDtypeStruct((2, n * shots, cols), jnp.bfloat16),
        in_specs=[pl.BlockSpec(memory_space=pl.ANY), smem, smem, smem, vmem, smem],
        out_specs=vmem,
        scratch_shapes=[
            pltpu.VMEM((2 * n, length), jnp.float32),
            pltpu.VMEM((SLOTS, cols, length), jnp.float32),
            pltpu.VMEM(block, jnp.float32),
            pltpu.VMEM(block, jnp.float32),
            pltpu.VMEM(block, jnp.float32),
            pltpu.VMEM((2, n * shots, cols), jnp.float32),
            pltpu.VMEM((2, n * shots, cols), jnp.float32),
            pltpu.SemaphoreType.DMA((SLOTS,)),
            pltpu.SemaphoreType.DMA((parts, n - 1)),
            pltpu.SemaphoreType.DMA((parts, n - 1)),
            pltpu.SemaphoreType.DMA((parts,)),
            pltpu.SemaphoreType.DMA((parts,)),
            pltpu.SemaphoreType.DMA((parts,)),
        ],
        compiler_params=pltpu.CompilerParams(
            collective_id=0, has_side_effects=True, vmem_limit_bytes=56 * 1024 * 1024),
        cost_estimate=pl.CostEstimate(flops=2 * 10**10, bytes_accessed=4 * shots * cols * length, transcendentals=0),
    )(traces, win_start, win_stop, shot_live, recv_live[None, :], band_start)
    return out[:, None]


def solution(mesh):
    placed = (
        P(("lines", "freq"), "rows", None),
        P(("lines", "freq")),
        P(("lines", "freq")),
        P(("lines", "freq")),
        P(("lines", "rows")),
        P("lines"),
    )
    return jax.shard_map(
        shards,
        mesh=mesh,
        in_specs=placed,
        out_specs=P(None, ("lines", "freq"), None, "rows"),
        check_vma=False,
    )
```

```python
import functools
import math

import jax
import jax.numpy as jnp
from jax import lax
from jax.experimental import pallas as pl
from jax.experimental.pallas import tpu as pltpu
from jax.sharding import PartitionSpec as P

RAMP = 32
SLOTS = 8
LAG = 3
MESH = pl.DeviceIdType.MESH


def split(x):
    high = x.astype(jnp.bfloat16)
    return high, (x - high.astype(jnp.float32)).astype(jnp.bfloat16)


def kernel(n, chunk, traces, win_start, win_stop, shot_live, recv_live, band_start, out, waves, slots, send, held, other, own, sib,
           slot_sem, send_sem, recv_sem, keep_sem, pass_sem, take_sem):
    me = lax.axis_index("freq")
    core = lax.axis_index("rows")
    shots, cols, length = traces.shape
    parts = shots // chunk

    def fetch(s):
        slot = lax.rem(s, SLOTS)
        return pltpu.make_async_copy(traces.at[s], slots.at[slot], slot_sem.at[slot])

    def remote(c, p):
        to = lax.rem(me + p, n)
        rows = pl.ds(c * chunk, chunk)
        return pltpu.make_async_remote_copy(
            send.at[:, to, rows, :], held.at[:, me, rows, :],
            send_sem.at[c, p - 1], recv_sem.at[c, p - 1],
            device_id={"freq": to}, device_id_type=MESH)

    def arrival(c, p):
        source = lax.rem(me + n - p, n)
        rows = pl.ds(c * chunk, chunk)
        return pltpu.make_async_remote_copy(
            send.at[:, source, rows, :], held.at[:, source, rows, :],
            send_sem.at[c, p - 1], recv_sem.at[c, p - 1],
            device_id={"freq": source}, device_id_type=MESH)

    def keep(c):
        rows = pl.ds(c * chunk, chunk)
        return pltpu.make_async_copy(send.at[:, me, rows, :], held.at[:, me, rows, :], keep_sem.at[c])

    def hand(c):
        rows = pl.ds(c * chunk, chunk)
        return pltpu.make_async_remote_copy(
            held.at[:, :, rows, :], other.at[:, :, rows, :], pass_sem.at[c], take_sem.at[c],
            device_id={"rows": 1 - core}, device_id_type=MESH)

    def hand_over(c):
        def land(p, carry):
            arrival(c, p).wait_recv()
            return carry
        lax.fori_loop(1, n, land, 0)
        keep(c).wait()
        hand(c).start()

    for s in range(min(SLOTS, shots)):
        fetch(s).start()

    row = lax.broadcasted_iota(jnp.int32, (2 * n, length), 0)
    times = lax.broadcasted_iota(jnp.int32, (2 * n, length), 1)
    sine = row >= n
    freqs = (band_start[0] + row - jnp.where(sine, n, 0)) & (length - 1)
    turns = (freqs * times + jnp.where(sine, length // 4, 0)) & (length - 1)
    waves[...] = jnp.cos(turns.astype(jnp.float32) * (2.0 * math.pi / length)) * (1.0 / math.sqrt(length))
    live = recv_live[...].astype(jnp.float32)
    clock = lax.broadcasted_iota(jnp.int32, (1, length), 1)

    barrier = pltpu.get_barrier_semaphore()

    def greet(p, carry):
        pl.semaphore_signal(barrier, inc=1, device_id={"freq": lax.rem(me + p, n)}, device_id_type=MESH)
        return carry
    lax.fori_loop(1, n, greet, 0)
    pl.semaphore_signal(barrier, inc=1, device_id={"rows": 1 - core}, device_id_type=MESH)

    def transform(s, carry):
        fetch(s).wait()
        slot = lax.rem(s, SLOTS)
        total = jnp.zeros((4 * n, cols), jnp.float32)
        rise = jnp.clip((clock - win_start[s]).astype(jnp.float32) * (1.0 / RAMP), 0.0, 1.0)
        fall = jnp.clip((win_stop[s] - clock).astype(jnp.float32) * (1.0 / RAMP), 0.0, 1.0)
        weight = rise * fall * shot_live[s].astype(jnp.float32)
        table = jnp.concatenate(split(waves[...] * weight), 0)
        step = 256
        for k in range(0, length, step):
            part = table[:, k:k + step]
            for piece in split(slots[slot, :, k:k + step]):
                total += lax.dot_general(part, piece, (((1,), (1,)), ((), ())),
                                         preferred_element_type=jnp.float32)
        spec = (total[:2 * n] + total[2 * n:]) * live
        for j in range(2 * n):
            send[j // n, j % n, pl.ds(s, 1), :] = spec[j:j + 1, :]

        @pl.when(s + SLOTS < shots)
        def _():
            fetch(s + SLOTS).start()
        return carry

    for c in range(parts):
        lax.fori_loop(c * chunk, (c + 1) * chunk, transform, 0)
        if c == 0:
            pl.semaphore_wait(barrier, n)

        def launch(i, carry):
            remote(c, lax.rem(i - 1 + core * (n // 2 - 1), n - 1) + 1).start()
            return carry
        lax.fori_loop(1, n, launch, 0)
        keep(c).start()
        if c >= LAG:
            hand_over(c - LAG)
    for c in range(max(parts - LAG, 0), parts):
        hand_over(c)

    def place(source_ref, target):
        for w in range(2):
            for source in range(n):
                target[w, source * shots:(source + 1) * shots, :] = source_ref[w, source]

    place(held, own)
    for c in range(parts):
        hand(c).wait_recv()
    place(other, sib)

    total_rows = n * shots
    scale = 1.0 / math.sqrt(total_rows)
    factors = []
    for half in (core, 1 - core):
        start = pl.multiple_of(half * cols, cols)
        right = jnp.concatenate([own[w, pl.ds(start, cols), :] for w in range(2)], 1)
        factors.append(split(right))
    tile = 128

    def multiply(i, carry):
        rows = pl.ds(pl.multiple_of(i * tile, tile), tile)
        sums = []
        for w in range(2):
            acc = jnp.zeros((tile, 2 * cols), jnp.float32)
            for ref, (right_high, right_low) in zip((own, sib), factors):
                high, low = split(ref[w, rows, :])
                acc += jnp.dot(high, right_high, preferred_element_type=jnp.float32)
                acc += jnp.dot(high, right_low, preferred_element_type=jnp.float32)
                acc += jnp.dot(low, right_high, preferred_element_type=jnp.float32)
            sums.append(acc)
        out[0, rows, :] = ((sums[0][:, :cols] - sums[1][:, cols:]) * scale).astype(out.dtype)
        out[1, rows, :] = ((sums[0][:, cols:] + sums[1][:, :cols]) * scale).astype(out.dtype)
        return carry
    lax.fori_loop(0, total_rows // tile, multiply, 0)

    for c in range(parts):
        def sent(p, carry):
            remote(c, p).wait_send()
            return carry
        lax.fori_loop(1, n, sent, 0)
        hand(c).wait_send()


def shards(traces, win_start, win_stop, shot_live, recv_live, band_start):
    shots, cols, length = traces.shape
    n = lax.axis_size("freq")
    chunk = min(8, shots)
    parts = shots // chunk
    block = (2, n, shots, cols)
    vmem = pl.BlockSpec(memory_space=pltpu.VMEM)
    smem = pl.BlockSpec(memory_space=pltpu.SMEM)
    out = pl.pallas_call(
        functools.partial(kernel, n, chunk),
        out_shape=jax.ShapeDtypeStruct((2, n * shots, cols), jnp.bfloat16),
        in_specs=[pl.BlockSpec(memory_space=pl.ANY), smem, smem, smem, vmem, smem],
        out_specs=vmem,
        scratch_shapes=[
            pltpu.VMEM((2 * n, length), jnp.float32),
            pltpu.VMEM((SLOTS, cols, length), jnp.float32),
            pltpu.VMEM(block, jnp.float32),
            pltpu.VMEM(block, jnp.float32),
            pltpu.VMEM(block, jnp.float32),
            pltpu.VMEM((2, n * shots, cols), jnp.float32),
            pltpu.VMEM((2, n * shots, cols), jnp.float32),
            pltpu.SemaphoreType.DMA((SLOTS,)),
            pltpu.SemaphoreType.DMA((parts, n - 1)),
            pltpu.SemaphoreType.DMA((parts, n - 1)),
            pltpu.SemaphoreType.DMA((parts,)),
            pltpu.SemaphoreType.DMA((parts,)),
            pltpu.SemaphoreType.DMA((parts,)),
        ],
        compiler_params=pltpu.CompilerParams(
            collective_id=0, has_side_effects=True, vmem_limit_bytes=56 * 1024 * 1024),
        cost_estimate=pl.CostEstimate(flops=2 * 10**10, bytes_accessed=4 * shots * cols * length, transcendentals=0),
    )(traces, win_start, win_stop, shot_live, recv_live[None, :], band_start)
    return out[:, None]


def solution(mesh):
    placed = (
        P(("lines", "freq"), "rows", None),
        P(("lines", "freq")),
        P(("lines", "freq")),
        P(("lines", "freq")),
        P(("lines", "rows")),
        P("lines"),
    )
    return jax.shard_map(
        shards,
        mesh=mesh,
        in_specs=placed,
        out_specs=P(None, ("lines", "freq"), None, "rows"),
        check_vma=False,
    )
```
